32 devices in a mesh: section: 2 (over core), seq: 4 (over z), wt: 4 (over y, x).
Axes of the slice: x: 2, y: 2, z: 4, core: 2. Of those that a mesh axis runs over, the one named last changes fastest.
Arguments:
- tokens: bfloat16 [2, 4, 1024, 1024], P(None, 'wt', 'seq'), may hold values from -6 to 6
- cotangent: bfloat16 [2, 4, 1024, 1024], P(None, 'wt', 'seq'), may hold values from -6 to 6
- in_weight: bfloat16 [2, 1024, 4384], P('section', 'wt'), may hold values from -0.1875 to 0.1875
- out_weight: bfloat16 [2, 2048, 1024], P('section', 'wt'), may hold values from -0.125 to 0.125
- conv_weight: bfloat16 [2, 4, 2304], P('section', None, 'wt'), may hold values from -3 to 3
- conv_bias: bfloat16 [2, 2304], P('section', 'wt'), may hold values from -0.5 to 0.5
- a_log: bfloat16 [2, 32], P('section', 'wt'), may hold values from -6 to 0
- dt_bias: bfloat16 [2, 32], P('section', 'wt'), may hold values from -4 to -1
- d_skip: bfloat16 [2, 32], P('section', 'wt'), may hold values from 0.5 to 1.5
- gain_in: bfloat16 [2, 1024], P('section', 'wt'), may hold values from 0.5 to 1.5
- gain_out: bfloat16 [2, 2048], P('section', 'wt'), may hold values from 0.5 to 1.5
Outputs:
- states: bfloat16 [2, 2, 4, 1024, 1024], P('section', None, 'wt', 'seq')
- input_grads: bfloat16 [2, 2, 4, 1024, 1024], P('section', None, 'wt', 'seq')
- grad_in_weight: float32 [2, 1024, 4384], P('section', 'wt')
- grad_out_weight: float32 [2, 2048, 1024], P('section', 'wt')
- grad_conv_weight: float32 [2, 4, 2304], P('section', None, 'wt')
- grad_conv_bias: float32 [2, 2304], P('section', 'wt')
- grad_a_log: float32 [2, 32], P('section', 'wt')
- grad_dt_bias: float32 [2, 32], P('section', 'wt')
- grad_d_skip: float32 [2, 32], P('section', 'wt')
- grad_gain_in: float32 [2, 1024], P('section', 'wt')
- grad_gain_out: float32 [2, 2048], P('section', 'wt')
The draws below stay inside these ranges and needn't reach their ends.
All inputs are finite; a program needn't handle non-finite values.
Results may differ from the reference program's by a relative error of at most 0.019.
Values may be sent and summed in bfloat16 or wider, within the bound.
A program may use at most 448 MiB of HBM per device.

```python
from functools import partial
import jax
import jax.numpy as jnp
from jax import lax

D = 1024
DI = 2048
NH = 32
KCONV = 4
BLOCK = 256
CONV = 2304
EXT = 4384
MB = 2
SEQ_LEN = 1024
SEQS = 4


def block_levels(stream_key, dims, shards, least, largest):
    level, own = 1.0, jax.random.fold_in(stream_key, 6)
    for axis_at, shards_of in shards:
        draws = jnp.exp(jax.random.uniform(jax.random.fold_in(own, axis_at), (shards_of,), jnp.float32, least / len(shards), largest / len(shards)))
        level = level * jnp.repeat(draws, dims[axis_at] // shards_of).reshape([-1 if axis == axis_at else 1 for axis in range(len(dims))])
    return level


def noise(key, dims, deviation, reach, shards=(), kind=jnp.bfloat16):
    loudness = block_levels(key, dims, shards, -0.22, 0.18) if shards else 1.0
    result = jax.random.normal(key, dims, jnp.float32) * deviation * loudness
    return jnp.minimum(jnp.maximum(result, -reach), reach).astype(kind)


def setup_inputs(seed: int = 0) -> dict:
    streams_of = jax.random.split(jax.random.key(seed), 12)
    return {
        "tokens": noise(streams_of[0], (MB, SEQS, SEQ_LEN, D), 1.0, 6.0, ((1, 4), (2, 4))),
        "cotangent": noise(streams_of[1], (MB, SEQS, SEQ_LEN, D), 1.0, 6.0, ((1, 4), (2, 4))),
        "in_weight": noise(streams_of[2], (2, D, EXT), D ** -0.5, 0.1875, ((0, 2), (1, 4))),
        "out_weight": noise(streams_of[3], (2, DI, D), DI ** -0.5, 0.125, ((0, 2), (1, 4))),
        "conv_weight": noise(streams_of[4], (2, KCONV, CONV), KCONV ** -0.5, 3.0, ((0, 2), (2, 4))),
        "conv_bias": jnp.clip(jax.random.uniform(streams_of[5], (2, CONV), jnp.float32, -0.5, 0.5) * block_levels(streams_of[5], (2, CONV), ((0, 2), (1, 4)), -0.4, 0.0), -0.5, 0.5).astype(jnp.bfloat16),
        "a_log": jnp.clip(-6.0 + 6.0 * jax.random.uniform(streams_of[6], (2, NH), jnp.float32) ** block_levels(streams_of[6], (2, NH), ((0, 2), (1, 4)), -0.2, 0.2), -6.0, 0.0).astype(jnp.bfloat16),
        "dt_bias": jnp.clip(-4.0 + 3.0 * jax.random.uniform(streams_of[7], (2, NH), jnp.float32) ** block_levels(streams_of[7], (2, NH), ((0, 2), (1, 4)), -0.2, 0.2), -4.0, -1.0).astype(jnp.bfloat16),
        "d_skip": jnp.clip(0.5 + 1.0 * jax.random.uniform(streams_of[8], (2, NH), jnp.float32) ** block_levels(streams_of[8], (2, NH), ((0, 2), (1, 4)), -0.2, 0.2), 0.5, 1.5).astype(jnp.bfloat16),
        "gain_in": jnp.clip(1.0 + 0.1 * jax.random.normal(streams_of[9], (2, D), jnp.float32), 0.5, 1.5).astype(jnp.bfloat16),
        "gain_out": jnp.clip(1.0 + 0.1 * jax.random.normal(streams_of[10], (2, DI), jnp.float32), 0.5, 1.5).astype(jnp.bfloat16),
    }


EPSILON = 1e-05
HIGH = lax.Precision.HIGHEST

@jax.custom_vjp
def low(v):
    return lax.optimization_barrier(v.astype(jnp.bfloat16)).astype(jnp.float32)

@jax.custom_vjp
def low_back(v):
    return v

def low_keep(v):
    return (low(v), None)

def low_pass(kept, grad):
    return (grad,)

def back_keep(v):
    return (v, None)

def back_low(kept, grad):
    return (low(grad),)
low.defvjp(low_keep, low_pass)
low_back.defvjp(back_keep, back_low)

def rms_scale(values, gain):
    return values * lax.rsqrt(lax.optimization_barrier(jnp.mean(values * values, axis=-1, keepdims=True)) + EPSILON) * gain

def causal_conv(inputs, kernel, offset_bias):
    taps_count = kernel.shape[0]
    length = inputs.shape[-2]
    padding = [(0, 0)] * (inputs.ndim - 2) + [(taps_count - 1, 0), (0, 0)]
    padded = jnp.pad(inputs, padding)
    accumulated = offset_bias
    for offset in range(taps_count):
        accumulated = accumulated + kernel[offset] * padded[..., offset:offset + length, :]
    return jax.nn.silu(accumulated)

def state_space(inputs, deltas, rates, b_rows, c_rows, block):
    length, head_count, head_size = inputs.shape
    blocks = length // block
    logdecay = (deltas * rates).reshape(blocks, block, head_count)
    scaled = (inputs * deltas[..., None]).reshape(blocks, block, head_count, head_size)
    b_blocks = b_rows.reshape(blocks, block, -1)
    c_blocks = c_rows.reshape(blocks, block, -1)
    cumulative = jnp.cumsum(logdecay, axis=1)
    gram_matrix = jnp.einsum('kin,kjn->kij', c_blocks, b_blocks, precision=HIGH)
    spread = cumulative[:, :, None, :] - cumulative[:, None, :, :]
    causal = (jnp.arange(block)[:, None] >= jnp.arange(block)[None, :])[None, :, :, None]
    weights = jnp.where(causal, jnp.exp(jnp.minimum(spread, 0.0)), 0.0) * gram_matrix[..., None]
    within = jnp.einsum('kijh,kjhp->kihp', weights, scaled, precision=HIGH)
    to_end = jnp.exp(cumulative[:, -1:, :] - cumulative)
    contrib = jnp.einsum('kjn,kjhp->khnp', b_blocks, scaled * to_end[..., None], precision=HIGH)
    totals = cumulative[:, -1, :]

    def advance(state_now, element):
        contrib_k, total_k = element
        return (jnp.exp(total_k)[:, None, None] * state_now + contrib_k, state_now)
    initial = jnp.zeros(contrib.shape[1:], inputs.dtype)
    unused_final, entering = lax.scan(advance, initial, (contrib, totals))
    across = jnp.einsum('kin,khnp->kihp', c_blocks, entering, precision=HIGH) * jnp.exp(cumulative)[..., None]
    return (within + across).reshape(length, head_count, head_size)

def mixer_layer(hidden, params):
    in_weight, out_weight, conv_weight, conv_bias, a_log, dt_bias, d_skip, gain_in, gain_out = params
    inner = out_weight.shape[0]
    state_size = (conv_weight.shape[1] - inner) // 2
    head_count = a_log.shape[0]
    head_size = inner // head_count
    normed = low(rms_scale(hidden, gain_in))
    project = low_back(jnp.dot(normed, in_weight, precision=HIGH))
    gate_part = project[:, :inner]
    x_part = low(project[:, inner:2 * inner])
    bc_part = low(project[:, 2 * inner:2 * inner + 2 * state_size])
    dt_part = low(project[:, 2 * inner + 2 * state_size:])
    convolved = causal_conv(jnp.concatenate([x_part, bc_part], axis=-1), conv_weight, conv_bias)
    x_heads = convolved[:, :inner].reshape(-1, head_count, head_size)
    b_rows = convolved[:, inner:inner + state_size]
    c_rows = convolved[:, inner + state_size:]
    deltas = jax.nn.softplus(dt_part + dt_bias)
    rates = -jnp.exp(a_log)
    mixed = state_space(x_heads, deltas, rates, b_rows, c_rows, BLOCK) + d_skip[:, None] * x_heads
    mixed = low_back(low(mixed.reshape(-1, inner)))
    scaled_out = low(rms_scale(mixed * jax.nn.silu(gate_part), gain_out))
    branch = low_back(jnp.dot(scaled_out, out_weight, precision=HIGH))
    return hidden + branch

def two_layers(inputs, probe_add, params):
    layers = [tuple((weight_array[layer_index] for weight_array in params)) for layer_index in range(2)]
    first_out = lax.map(jax.checkpoint(partial(mixer_layer, params=layers[0])), inputs)
    middle = low_back(low(first_out))
    second = lax.map(jax.checkpoint(partial(mixer_layer, params=layers[1])), middle + probe_add)
    return (middle, second)

def reference(tokens, cotangent, in_weight, out_weight, conv_weight, conv_bias, a_log, dt_bias, d_skip, gain_in, gain_out):
    inputs = tokens.astype(jnp.float32).reshape(-1, SEQ_LEN, D)
    upstream = cotangent.astype(jnp.float32).reshape(-1, SEQ_LEN, D)
    params = tuple((weight_array.astype(jnp.float32) for weight_array in (in_weight, out_weight, conv_weight, conv_bias, a_log, dt_bias, d_skip, gain_in, gain_out)))
    outcome, pullback = jax.vjp(two_layers, inputs, jnp.zeros_like(inputs), params)
    middle, second = outcome
    grad_inputs, grad_probe, grad_params = pullback((jnp.zeros_like(middle), upstream))
    states = jnp.stack([middle, second]).reshape(2, MB, SEQS, SEQ_LEN, D).astype(jnp.bfloat16)
    input_grads = jnp.stack([grad_inputs, grad_probe]).reshape(2, MB, SEQS, SEQ_LEN, D).astype(jnp.bfloat16)
    return (states, input_grads, grad_params[0], grad_params[1], grad_params[2], grad_params[3], grad_params[4], grad_params[5], grad_params[6], grad_params[7], grad_params[8])
```

```python
import jax
import jax.numpy as jnp
from jax import lax
from jax.experimental import pallas as pl
from jax.experimental.pallas import tpu as pltpu
from jax.sharding import PartitionSpec as P

EPSILON = 1e-05
HIGH = lax.Precision.HIGHEST
F32 = jnp.float32
BF16 = jnp.bfloat16
LANES = 128


def shifted(block, axis, distance):
    devices = range(lax.axis_size(axis))
    route = [(i - distance, i) for i in devices if i - distance in devices]
    return lax.ppermute(block, axis, route)


def swapped(block):
    return lax.ppermute(block, "section", [(0, 1), (1, 0)])


def rms_scale(values, gain):
    return values * lax.rsqrt(jnp.mean(values * values, axis=-1, keepdims=True) + EPSILON) * gain


def post_norm(mixed, gate_part, gain_out):
    return rms_scale(mixed * jax.nn.silu(gate_part), gain_out)


def dot(a, b, over):
    return lax.dot_general(
        a.astype(BF16), b.astype(BF16), (over, ((), ())), preferred_element_type=F32
    )


ROWS_COLS = ((1,), (0,))
COLS_COLS = ((1,), (1,))
ROWS_ROWS = ((0,), (0,))


def head_decay(head, cum_ref, cum_t_ref):
    heads = lax.broadcasted_iota(jnp.int32, cum_ref.shape, 1)
    column = jnp.sum(jnp.where(heads == head, cum_ref[...], 0.0), axis=1, keepdims=True)
    row = cum_t_ref[pl.ds(head, 1), :]
    return jnp.exp(jnp.minimum(column - row, 0.0))


def causal_gram(c_ref, b_ref, gram):
    length = gram.shape[0]
    product = dot(c_ref[...], b_ref[...], COLS_COLS)
    rows = lax.broadcasted_iota(jnp.int32, (length, length), 0)
    cols = lax.broadcasted_iota(jnp.int32, (length, length), 1)
    gram[...] = jnp.where(rows >= cols, product, 0.0)


def within_kernel(head_size, u_ref, cum_ref, cum_t_ref, b_ref, c_ref, y_ref, gram):
    tile = pl.program_id(0)
    per_tile = LANES // head_size

    @pl.when(tile == 0)
    def _():
        causal_gram(c_ref, b_ref, gram)

    u = u_ref[...]
    owner = lax.broadcasted_iota(jnp.int32, u.shape, 1) // head_size
    total = jnp.zeros(u.shape, F32)
    for k in range(per_tile):
        weights = head_decay(tile * per_tile + k, cum_ref, cum_t_ref) * gram[...]
        total += dot(weights, jnp.where(owner == k, u, 0.0), ROWS_COLS)
    y_ref[...] = total


def within_back_kernel(
    head_size,
    u_ref,
    dy_ref,
    cum_ref,
    cum_t_ref,
    b_ref,
    c_ref,
    du_ref,
    dgram_ref,
    rows_ref,
    cols_ref,
    gram,
):
    tile = pl.program_id(0)
    per_tile = LANES // head_size

    @pl.when(tile == 0)
    def _():
        causal_gram(c_ref, b_ref, gram)
        dgram_ref[...] = jnp.zeros_like(dgram_ref)
        rows_ref[...] = jnp.zeros_like(rows_ref)

    u = u_ref[...].astype(BF16)
    dy = dy_ref[...]
    length = u.shape[0]
    owner = lax.broadcasted_iota(jnp.int32, dy.shape, 1) // head_size
    heads = lax.broadcasted_iota(jnp.int32, rows_ref.shape, 1)
    causal = lax.broadcasted_iota(jnp.int32, (length, length), 0) >= lax.broadcasted_iota(
        jnp.int32, (length, length), 1
    )
    total = jnp.zeros(dy.shape, F32)
    for k in range(per_tile):
        head = tile * per_tile + k
        decay = head_decay(head, cum_ref, cum_t_ref)
        weights = decay * gram[...]
        dy_own = jnp.where(owner == k, dy, 0.0).astype(BF16)
        dweights = dot(dy_own, u, COLS_COLS)
        dgram_ref[...] += jnp.where(causal, dweights * decay, 0.0)
        pairs = dweights * weights
        rows_ref[...] += jnp.where(heads == head, jnp.sum(pairs, axis=1, keepdims=True), 0.0)
        cols_ref[pl.ds(head, 1), :] = jnp.sum(pairs, axis=0, keepdims=True)
        total += dot(weights, dy_own, ROWS_ROWS)
    du_ref[...] = total


def full(shape):
    return pl.BlockSpec(shape, lambda i: (0,) * len(shape))


def within(u, cum, b, c, head_size):
    length, channels = u.shape
    cum_t = cum.T
    tile = pl.BlockSpec((length, LANES), lambda i: (0, i))
    return pl.pallas_call(
        lambda *refs: within_kernel(head_size, *refs),
        grid=(channels // LANES,),
        out_shape=jax.ShapeDtypeStruct(u.shape, F32),
        in_specs=[tile, full(cum.shape), full(cum_t.shape), full(b.shape), full(c.shape)],
        out_specs=tile,
        scratch_shapes=[pltpu.VMEM((length, length), F32)],
        cost_estimate=pl.CostEstimate(
            flops=length * length * channels * 8,
            bytes_accessed=8 * u.size,
            transcendentals=length * length * channels // head_size,
        ),
    )(u, cum, cum_t, b, c)


def within_back(u, dy, cum, b, c, head_size):
    length, channels = u.shape
    cum_t = cum.T
    tile = pl.BlockSpec((length, LANES), lambda i: (0, i))
    return pl.pallas_call(
        lambda *refs: within_back_kernel(head_size, *refs),
        grid=(channels // LANES,),
        out_shape=(
            jax.ShapeDtypeStruct(u.shape, F32),
            jax.ShapeDtypeStruct((length, length), F32),
            jax.ShapeDtypeStruct(cum.shape, F32),
            jax.ShapeDtypeStruct(cum_t.shape, F32),
        ),
        in_specs=[tile, tile, full(cum.shape), full(cum_t.shape), full(b.shape), full(c.shape)],
        out_specs=(tile, full((length, length)), full(cum.shape), full(cum_t.shape)),
        scratch_shapes=[pltpu.VMEM((length, length), F32)],
        cost_estimate=pl.CostEstimate(
            flops=length * length * channels * 16,
            bytes_accessed=12 * u.size,
            transcendentals=length * length * channels // head_size,
        ),
    )(u, dy, cum, cum_t, b, c)


def carried(term, decay, distance):
    count = lax.axis_size("seq")
    if count == 1:
        return jnp.zeros_like(term)
    state = shifted(term.astype(BF16), "seq", distance).astype(F32)
    for _ in range(count - 2):
        state = shifted((term + decay * state).astype(BF16), "seq", distance).astype(F32)
    return state


def split_halves(array, parts, first):
    share = array.shape[1] // (2 * parts)
    pieces = [array[:, j * share : (j + 1) * share] for j in range(2 * parts)]
    even = jnp.concatenate(pieces[0::2], axis=1)
    odd = jnp.concatenate(pieces[1::2], axis=1)
    return jnp.where(first, even, odd), jnp.where(first, odd, even)


def join_halves(mine, other, parts, first):
    even, odd = jnp.where(first, mine, other), jnp.where(first, other, mine)
    share = mine.shape[1] // parts
    pieces = []
    for j in range(parts):
        pieces += [even[:, j * share : (j + 1) * share], odd[:, j * share : (j + 1) * share]]
    return jnp.concatenate(pieces, axis=1)


def head_map(heads, channels):
    return (jnp.arange(channels)[None, :] // (channels // heads) == jnp.arange(heads)[:, None]).astype(F32)


def layer_forward(hidden_b, weights, small, first, parts):
    (win_mine, win_other), (wout_mine, wout_other) = weights
    conv_weight, conv_bias, a_log, dt_bias, d_skip, gain_in, gain_out = small
    heads, inner, conv = a_log.shape[0], gain_out.shape[0], conv_bias.shape[0]
    head_size = inner // heads
    state_size = (conv - inner) // 2
    taps = conv_weight.shape[0]
    hidden = hidden_b.astype(F32)
    length = hidden.shape[0]
    normed = rms_scale(hidden, gain_in).astype(BF16)
    normed_mine, normed_other = split_halves(normed, parts, first)
    project = dot(normed_mine, win_mine, ROWS_COLS) + dot(normed_other, win_other, ROWS_COLS)
    gate = project[:, :inner]
    v = project[:, inner : inner + conv].astype(BF16)
    dt_raw = project[:, inner + conv :].astype(BF16).astype(F32)
    halo = shifted(v[length - taps + 1 :], "seq", 1)
    padded = jnp.concatenate([halo, v], axis=0).astype(F32)
    pre = conv_bias
    for k in range(taps):
        pre = pre + conv_weight[k] * padded[k : k + length]
    conv_out = jax.nn.silu(pre)
    xs = conv_out[:, :inner]
    b = conv_out[:, inner : inner + state_size]
    c = conv_out[:, inner + state_size :]
    delta = jax.nn.softplus(dt_raw + dt_bias)
    rate = -jnp.exp(a_log)
    tri = jnp.tril(jnp.ones((length, length), F32))
    cum = jnp.dot(tri, delta * rate, precision=HIGH)
    last = cum[length - 1 :]
    widen = head_map(heads, inner)
    delta_w = jnp.dot(delta, widen, precision=HIGH)
    cum_w = jnp.dot(jnp.exp(cum), widen, precision=HIGH)
    end_w = jnp.dot(jnp.exp(last - cum), widen, precision=HIGH)
    decay = cum_w[length - 1 :]
    skip_w = jnp.repeat(d_skip, head_size)
    u = xs * delta_w
    term = dot(b, u * end_w, ROWS_ROWS)
    entering = carried(term, decay, 1)
    inside = within(u, cum, b, c, head_size)
    across = cum_w * dot(c, entering, ROWS_COLS)
    mixed = (inside + across + skip_w * xs).astype(BF16)
    scaled = post_norm(mixed.astype(F32), gate, gain_out).astype(BF16)
    scaled_mine, scaled_other = split_halves(scaled, parts, first)
    output = (
        hidden
        + dot(scaled_mine, wout_mine, ROWS_COLS)
        + dot(scaled_other, wout_other, ROWS_COLS)
    )
    saved = (
        hidden, normed_mine, normed_other, gate, padded, dt_raw, pre, xs, b, c, delta, rate, tri,
        cum, widen, delta_w, cum_w, end_w, decay, skip_w, u, entering, across, mixed,
        scaled_mine, scaled_other,
    )
    return output.astype(BF16), saved


def layer_backward(upstream_b, saved, weights, small, first, parts):
    (win_mine, win_other), (wout_mine, wout_other) = weights
    conv_weight, conv_bias, a_log, dt_bias, d_skip, gain_in, gain_out = small
    (
        hidden, normed_mine, normed_other, gate, padded, dt_raw, pre, xs, b, c, delta, rate, tri,
        cum, widen, delta_w, cum_w, end_w, decay, skip_w, u, entering, across, mixed,
        scaled_mine, scaled_other,
    ) = saved
    heads, inner = a_log.shape[0], gain_out.shape[0]
    head_size = inner // heads
    taps = conv_weight.shape[0]
    length = hidden.shape[0]

    def narrow(array):
        return dot(array, widen, COLS_COLS)

    grad_scaled = join_halves(
        dot(upstream_b, wout_mine, COLS_COLS), dot(upstream_b, wout_other, COLS_COLS), parts, first
    )
    grad_wout = (
        dot(scaled_mine, upstream_b, ROWS_ROWS),
        dot(scaled_other, upstream_b, ROWS_ROWS).astype(BF16),
    )
    _, post_pull = jax.vjp(post_norm, mixed.astype(F32), gate, gain_out)
    grad_mixed, grad_gate, grad_gain_out = post_pull(grad_scaled)
    dy = grad_mixed.astype(BF16).astype(F32)
    dy_cum = dy * cum_w
    a_term = dot(c, dy_cum, ROWS_ROWS)
    a_out = carried(a_term, decay, -1)
    du_inside, dgram, pair_rows, pair_cols = within_back(u, dy, cum, b, c, head_size)
    grad_c = dot(dy_cum, entering, COLS_COLS) + dot(dgram, b, ROWS_COLS)
    grad_b = dot(u * end_w, a_out, COLS_COLS) + dot(dgram, c, ROWS_ROWS)
    du_state = end_w * dot(b, a_out, ROWS_COLS)
    moved = narrow(du_state * u)
    decay_grad = jnp.sum(a_out * entering, axis=0, keepdims=True) * decay
    grad_last = jnp.sum(moved, axis=0, keepdims=True) + jnp.dot(
        decay_grad, widen.T, precision=HIGH
    )
    grad_cum = pair_rows - pair_cols.T + narrow(dy * across) - moved
    grad_log = lax.dot_general(tri, grad_cum, (ROWS_ROWS, ((), ())), precision=HIGH) + grad_last
    du = du_inside + du_state
    grad_xs = du * delta_w + skip_w * dy
    grad_delta = grad_log * rate + narrow(du * xs)
    grad_a_log = jnp.sum(grad_log * delta, axis=0) * rate
    grad_skip = jnp.dot(jnp.sum(dy * xs, axis=0), widen.T, precision=HIGH)
    grad_dt_raw = grad_delta * jax.nn.sigmoid(dt_raw + dt_bias)
    grad_dt_bias = jnp.sum(grad_dt_raw, axis=0)
    sig = jax.nn.sigmoid(pre)
    grad_pre = jnp.concatenate([grad_xs, grad_b, grad_c], axis=1) * sig * (1.0 + pre * (1.0 - sig))
    halo = shifted(grad_pre[: taps - 1].astype(BF16), "seq", -1).astype(F32)
    grad_padded = jnp.concatenate([grad_pre, halo], axis=0)
    grad_v = sum(
        conv_weight[k] * grad_padded[taps - 1 - k : taps - 1 - k + length] for k in range(taps)
    )
    grad_conv_weight = jnp.stack(
        [jnp.sum(grad_pre * padded[k : k + length], axis=0) for k in range(taps)]
    )
    grad_conv_bias = jnp.sum(grad_pre, axis=0)
    grad_project = jnp.concatenate(
        [grad_gate.astype(BF16), grad_v.astype(BF16), grad_dt_raw.astype(BF16)], axis=1
    )
    grad_normed = join_halves(
        dot(grad_project, win_mine, COLS_COLS),
        dot(grad_project, win_other, COLS_COLS),
        parts,
        first,
    )
    grad_win = (
        dot(normed_mine, grad_project, ROWS_ROWS),
        dot(normed_other, grad_project, ROWS_ROWS).astype(BF16),
    )
    _, norm_pull = jax.vjp(rms_scale, hidden, gain_in)
    grad_hidden, grad_gain_in = norm_pull(grad_normed)
    grad_small = (
        grad_conv_weight, grad_conv_bias, grad_a_log, grad_dt_bias, grad_skip, grad_gain_in,
        grad_gain_out,
    )
    return (upstream_b.astype(F32) + grad_hidden).astype(BF16), grad_win, grad_wout, grad_small


def reduced(grad):
    mine, other = grad
    both = (mine + swapped(other).astype(F32)).astype(BF16)
    share = lax.psum_scatter(both, "wt", scatter_dimension=0, tiled=True)
    return lax.psum(share, "seq")


def own_layer(layers, first):
    recv0 = lax.ppermute(layers[0], "section", [(1, 0)])
    recv1 = lax.ppermute(layers[1], "section", [(0, 1)])
    own = jnp.where(first, layers[0], layers[1])
    recv = jnp.where(first, recv0, recv1)
    joined = jnp.concatenate([jnp.where(first, own, recv), jnp.where(first, recv, own)], axis=0)
    return joined.astype(F32)[None]


def by_layer(results, first):
    own = jnp.where(first, results[0], results[1])
    recv = swapped(jnp.where(first, results[1], results[0]))
    return jnp.stack([jnp.where(first, own, recv), jnp.where(first, recv, own)])[None, :, None]


def local(tokens, cotangent, in_weight, out_weight, *small_shards):
    section = lax.axis_index("section")
    first = section == 0
    wt_id = lax.axis_index("wt")
    parts = lax.axis_size("wt")

    def halves(weight):
        rows = weight.shape[1] // 2
        keep = lax.dynamic_slice_in_dim(weight[0], section * rows, rows, 0)
        recv = swapped(lax.dynamic_slice_in_dim(weight[0], (1 - section) * rows, rows, 0))
        return jnp.where(first, keep, recv), jnp.where(first, recv, keep)

    def gathered(half):
        mine = lax.all_gather(half, "wt", axis=0, tiled=True)
        return mine, swapped(mine)

    win_halves, wout_halves = halves(in_weight), halves(out_weight)
    flat = jnp.concatenate([shard[0].reshape(-1) for shard in small_shards])
    packed = lax.all_gather(flat, ("section", "wt"), axis=0, tiled=False)
    packed = packed.reshape(2, parts, -1).astype(F32)
    smalls = []
    for layer in range(2):
        rest, small = packed[layer], []
        for shard in small_shards:
            shape = shard.shape[1:]
            size = shard[0].size
            piece, rest = rest[:, :size], rest[:, size:]
            if len(shape) == 2:
                piece = piece.reshape((parts,) + shape).swapaxes(0, 1)
                small.append(piece.reshape(shape[0], -1))
            else:
                small.append(piece.reshape(-1))
        smalls.append(tuple(small))
    win0 = gathered(win_halves[0])
    wout0 = gathered(wout_halves[0])
    win1 = gathered(win_halves[1])
    wout1 = gathered(wout_halves[1])
    weights = ((win0, wout0), (win1, wout1))

    own_tokens = lax.dynamic_index_in_dim(tokens, section, 0, keepdims=False)[0]
    own_cotangent = lax.dynamic_index_in_dim(cotangent, section, 0, keepdims=False)[0]
    out0, saved0 = layer_forward(own_tokens, weights[0], smalls[0], first, parts)
    out1, saved1 = layer_forward(out0, weights[1], smalls[1], first, parts)
    states = by_layer((out0, out1), first)
    back1, gwin1, gwout1, gsmall1 = layer_backward(
        own_cotangent, saved1, weights[1], smalls[1], first, parts
    )
    sum_wout1, sum_win1 = reduced(gwout1), reduced(gwin1)
    back0, gwin0, gwout0, gsmall0 = layer_backward(
        back1, saved0, weights[0], smalls[0], first, parts
    )
    sum_wout0, sum_win0 = reduced(gwout0), reduced(gwin0)
    input_grads = by_layer((back0, back1), first)

    flat0 = jnp.concatenate([g.reshape(-1) for g in gsmall0])
    flat1 = jnp.concatenate([g.reshape(-1) for g in gsmall1])
    total = jnp.where(first, flat0, flat1) + swapped(jnp.where(first, flat1, flat0))
    total = lax.psum(total, ("seq", "wt"))
    small_out, at = [], 0
    for g in gsmall0:
        piece = total[at : at + g.size].reshape(g.shape)
        at += g.size
        axis = g.ndim - 1
        share = g.shape[axis] // parts
        small_out.append(lax.dynamic_slice_in_dim(piece, wt_id * share, share, axis)[None])
    return (
        states,
        input_grads,
        own_layer((sum_win0, sum_win1), first),
        own_layer((sum_wout0, sum_wout1), first),
        *small_out,
    )


def solution(mesh):
    shards = (
        P("section", "wt", None),
        P("section", "wt", None),
        P("section", None, "wt"),
        P("section", "wt"),
        P("section", "wt"),
        P("section", "wt"),
        P("section", "wt"),
        P("section", "wt"),
        P("section", "wt"),
    )
    return jax.shard_map(
        local,
        mesh=mesh,
        in_specs=(P(None, "wt", "seq", None), P(None, "wt", "seq", None)) + shards,
        out_specs=(P("section", None, "wt", "seq", None), P("section", None, "wt", "seq", None))
        + shards,
        check_vma=False,
    )
```

```python
import jax
import jax.numpy as jnp
from jax import lax
from jax.experimental import pallas as pl
from jax.experimental.pallas import tpu as pltpu
from jax.sharding import PartitionSpec as P

EPSILON = 1e-05
HIGH = lax.Precision.HIGHEST
F32 = jnp.float32
BF16 = jnp.bfloat16
LANES = 128


def shifted(block, axis, distance):
    devices = range(lax.axis_size(axis))
    route = [(i - distance, i) for i in devices if i - distance in devices]
    return lax.ppermute(block, axis, route)


def swapped(block):
    return lax.ppermute(block, "section", [(0, 1), (1, 0)])


def crossed(block, axis, bit):
    devices = range(lax.axis_size(axis))
    return lax.ppermute(block, axis, [(i, i ^ bit) for i in devices])


def bits_of(axis):
    count = lax.axis_size(axis)
    return [1 << k for k in range(count.bit_length() - 1)]


def has_bit(axis, bit):
    return (lax.axis_index(axis) // bit) % 2 == 1


def gather_rows(block, axis, order):
    rows, columns = block.shape
    done = []
    for bit in order:
        recv, high = crossed(block, axis, bit), has_bit(axis, bit)
        at = sum(1 for other in done if other > bit)
        block = jnp.stack([jnp.where(high, recv, block), jnp.where(high, block, recv)], axis=at)
        done.append(bit)
    return block.reshape(-1, columns)


def scatter_rows(total, axis, order):
    rows, columns = total.shape
    left = sorted(order, reverse=True)
    total = total.reshape((2,) * len(left) + (rows >> len(left), columns))
    for bit in order:
        at = left.index(bit)
        left.remove(bit)
        low = lax.index_in_dim(total, 0, at, keepdims=False)
        top = lax.index_in_dim(total, 1, at, keepdims=False)
        high = has_bit(axis, bit)
        recv = crossed(jnp.where(high, low, top), axis, bit)
        total = (jnp.where(high, top, low).astype(F32) + recv.astype(F32)).astype(BF16)
    return total


def sum_rows(total, axis):
    order = bits_of(axis)
    return gather_rows(scatter_rows(total, axis, order), axis, order[::-1])


def rms_scale(values, gain):
    return values * lax.rsqrt(jnp.mean(values * values, axis=-1, keepdims=True) + EPSILON) * gain


def post_norm(mixed, gate_part, gain_out):
    return rms_scale(mixed * jax.nn.silu(gate_part), gain_out)


def dot(a, b, over):
    return lax.dot_general(
        a.astype(BF16), b.astype(BF16), (over, ((), ())), preferred_element_type=F32
    )


ROWS_COLS = ((1,), (0,))
COLS_COLS = ((1,), (1,))
ROWS_ROWS = ((0,), (0,))


def head_decay(head, cum_ref, cum_t_ref):
    heads = lax.broadcasted_iota(jnp.int32, cum_ref.shape, 1)
    column = jnp.sum(jnp.where(heads == head, cum_ref[...], 0.0), axis=1, keepdims=True)
    row = cum_t_ref[pl.ds(head, 1), :]
    return jnp.exp(jnp.minimum(column - row, 0.0))


def causal_gram(c_ref, b_ref, gram):
    length = gram.shape[0]
    product = dot(c_ref[...], b_ref[...], COLS_COLS)
    rows = lax.broadcasted_iota(jnp.int32, (length, length), 0)
    cols = lax.broadcasted_iota(jnp.int32, (length, length), 1)
    gram[...] = jnp.where(rows >= cols, product, 0.0)


def within_kernel(head_size, u_ref, cum_ref, cum_t_ref, b_ref, c_ref, y_ref, gram):
    tile = pl.program_id(0)
    per_tile = LANES // head_size

    @pl.when(tile == 0)
    def _():
        causal_gram(c_ref, b_ref, gram)

    u = u_ref[...]
    owner = lax.broadcasted_iota(jnp.int32, u.shape, 1) // head_size
    total = jnp.zeros(u.shape, F32)
    for k in range(per_tile):
        weights = head_decay(tile * per_tile + k, cum_ref, cum_t_ref) * gram[...]
        total += dot(weights, jnp.where(owner == k, u, 0.0), ROWS_COLS)
    y_ref[...] = total


def within_back_kernel(
    head_size,
    u_ref,
    dy_ref,
    cum_ref,
    cum_t_ref,
    b_ref,
    c_ref,
    du_ref,
    dgram_ref,
    rows_ref,
    cols_ref,
    gram,
):
    tile = pl.program_id(0)
    per_tile = LANES // head_size

    @pl.when(tile == 0)
    def _():
        causal_gram(c_ref, b_ref, gram)
        dgram_ref[...] = jnp.zeros_like(dgram_ref)
        rows_ref[...] = jnp.zeros_like(rows_ref)

    u = u_ref[...].astype(BF16)
    dy = dy_ref[...]
    length = u.shape[0]
    owner = lax.broadcasted_iota(jnp.int32, dy.shape, 1) // head_size
    heads = lax.broadcasted_iota(jnp.int32, rows_ref.shape, 1)
    causal = lax.broadcasted_iota(jnp.int32, (length, length), 0) >= lax.broadcasted_iota(
        jnp.int32, (length, length), 1
    )
    total = jnp.zeros(dy.shape, F32)
    for k in range(per_tile):
        head = tile * per_tile + k
        decay = head_decay(head, cum_ref, cum_t_ref)
        weights = decay * gram[...]
        dy_own = jnp.where(owner == k, dy, 0.0).astype(BF16)
        dweights = dot(dy_own, u, COLS_COLS)
        dgram_ref[...] += jnp.where(causal, dweights * decay, 0.0)
        pairs = dweights * weights
        rows_ref[...] += jnp.where(heads == head, jnp.sum(pairs, axis=1, keepdims=True), 0.0)
        cols_ref[pl.ds(head, 1), :] = jnp.sum(pairs, axis=0, keepdims=True)
        total += dot(weights, dy_own, ROWS_ROWS)
    du_ref[...] = total


def full(shape):
    return pl.BlockSpec(shape, lambda i: (0,) * len(shape))


def within(u, cum, b, c, head_size):
    length, channels = u.shape
    cum_t = cum.T
    tile = pl.BlockSpec((length, LANES), lambda i: (0, i))
    return pl.pallas_call(
        lambda *refs: within_kernel(head_size, *refs),
        grid=(channels // LANES,),
        out_shape=jax.ShapeDtypeStruct(u.shape, F32),
        in_specs=[tile, full(cum.shape), full(cum_t.shape), full(b.shape), full(c.shape)],
        out_specs=tile,
        scratch_shapes=[pltpu.VMEM((length, length), F32)],
        cost_estimate=pl.CostEstimate(
            flops=length * length * channels * 8,
            bytes_accessed=8 * u.size,
            transcendentals=length * length * channels // head_size,
        ),
    )(u, cum, cum_t, b, c)


def within_back(u, dy, cum, b, c, head_size):
    length, channels = u.shape
    cum_t = cum.T
    tile = pl.BlockSpec((length, LANES), lambda i: (0, i))
    return pl.pallas_call(
        lambda *refs: within_back_kernel(head_size, *refs),
        grid=(channels // LANES,),
        out_shape=(
            jax.ShapeDtypeStruct(u.shape, F32),
            jax.ShapeDtypeStruct((length, length), F32),
            jax.ShapeDtypeStruct(cum.shape, F32),
            jax.ShapeDtypeStruct(cum_t.shape, F32),
        ),
        in_specs=[tile, tile, full(cum.shape), full(cum_t.shape), full(b.shape), full(c.shape)],
        out_specs=(tile, full((length, length)), full(cum.shape), full(cum_t.shape)),
        scratch_shapes=[pltpu.VMEM((length, length), F32)],
        cost_estimate=pl.CostEstimate(
            flops=length * length * channels * 16,
            bytes_accessed=12 * u.size,
            transcendentals=length * length * channels // head_size,
        ),
    )(u, dy, cum, cum_t, b, c)


def carried(term, decay, distance):
    count = lax.axis_size("seq")
    if count == 1:
        return jnp.zeros_like(term)
    state = shifted(term.astype(BF16), "seq", distance).astype(F32)
    for _ in range(count - 2):
        state = shifted((term + decay * state).astype(BF16), "seq", distance).astype(F32)
    return state


def split_halves(array, parts, first):
    share = array.shape[1] // (2 * parts)
    pieces = [array[:, j * share : (j + 1) * share] for j in range(2 * parts)]
    even = jnp.concatenate(pieces[0::2], axis=1)
    odd = jnp.concatenate(pieces[1::2], axis=1)
    return jnp.where(first, even, odd), jnp.where(first, odd, even)


def join_halves(mine, other, parts, first):
    even, odd = jnp.where(first, mine, other), jnp.where(first, other, mine)
    share = mine.shape[1] // parts
    pieces = []
    for j in range(parts):
        pieces += [even[:, j * share : (j + 1) * share], odd[:, j * share : (j + 1) * share]]
    return jnp.concatenate(pieces, axis=1)


def head_map(heads, channels):
    return (jnp.arange(channels)[None, :] // (channels // heads) == jnp.arange(heads)[:, None]).astype(F32)


def layer_forward(hidden_b, weights, small, first, parts):
    (win_mine, win_other), (wout_mine, wout_other) = weights
    conv_weight, conv_bias, a_log, dt_bias, d_skip, gain_in, gain_out = small
    heads, inner, conv = a_log.shape[0], gain_out.shape[0], conv_bias.shape[0]
    head_size = inner // heads
    state_size = (conv - inner) // 2
    taps = conv_weight.shape[0]
    hidden = hidden_b.astype(F32)
    length = hidden.shape[0]
    normed = rms_scale(hidden, gain_in).astype(BF16)
    normed_mine, normed_other = split_halves(normed, parts, first)
    gate, project = (
        dot(normed_mine, mine, ROWS_COLS) + dot(normed_other, other, ROWS_COLS)
        for mine, other in zip(win_mine, win_other)
    )
    v = project[:, :conv].astype(BF16)
    dt_raw = project[:, conv:].astype(BF16).astype(F32)
    halo = shifted(v[length - taps + 1 :], "seq", 1)
    padded = jnp.concatenate([halo, v], axis=0).astype(F32)
    pre = conv_bias
    for k in range(taps):
        pre = pre + conv_weight[k] * padded[k : k + length]
    conv_out = jax.nn.silu(pre)
    xs = conv_out[:, :inner]
    b = conv_out[:, inner : inner + state_size]
    c = conv_out[:, inner + state_size :]
    delta = jax.nn.softplus(dt_raw + dt_bias)
    rate = -jnp.exp(a_log)
    tri = jnp.tril(jnp.ones((length, length), F32))
    cum = jnp.dot(tri, delta * rate, precision=HIGH)
    last = cum[length - 1 :]
    widen = head_map(heads, inner)
    delta_w = jnp.dot(delta, widen, precision=HIGH)
    cum_w = jnp.dot(jnp.exp(cum), widen, precision=HIGH)
    end_w = jnp.dot(jnp.exp(last - cum), widen, precision=HIGH)
    decay = cum_w[length - 1 :]
    skip_w = jnp.repeat(d_skip, head_size)
    u = xs * delta_w
    term = dot(b, u * end_w, ROWS_ROWS)
    entering = carried(term, decay, 1)
    inside = within(u, cum, b, c, head_size)
    across = cum_w * dot(c, entering, ROWS_COLS)
    mixed = (inside + across + skip_w * xs).astype(BF16)
    scaled = post_norm(mixed.astype(F32), gate, gain_out).astype(BF16)
    scaled_mine, scaled_other = split_halves(scaled, parts, first)
    output = (
        hidden
        + dot(scaled_mine, wout_mine, ROWS_COLS)
        + dot(scaled_other, wout_other, ROWS_COLS)
    )
    saved = (
        hidden, normed_mine, normed_other, gate, padded, dt_raw, pre, xs, b, c, delta, rate, tri,
        cum, widen, delta_w, cum_w, end_w, decay, skip_w, u, entering, across, mixed,
        scaled_mine, scaled_other,
    )
    return output.astype(BF16), saved


def layer_backward(upstream_b, saved, weights, small, first, parts):
    (win_mine, win_other), (wout_mine, wout_other) = weights
    conv_weight, conv_bias, a_log, dt_bias, d_skip, gain_in, gain_out = small
    (
        hidden, normed_mine, normed_other, gate, padded, dt_raw, pre, xs, b, c, delta, rate, tri,
        cum, widen, delta_w, cum_w, end_w, decay, skip_w, u, entering, across, mixed,
        scaled_mine, scaled_other,
    ) = saved
    heads, inner = a_log.shape[0], gain_out.shape[0]
    head_size = inner // heads
    taps = conv_weight.shape[0]
    length = hidden.shape[0]

    def narrow(array):
        return dot(array, widen, COLS_COLS)

    grad_scaled = join_halves(
        dot(upstream_b, wout_mine, COLS_COLS), dot(upstream_b, wout_other, COLS_COLS), parts, first
    )
    grad_wout = (
        dot(scaled_mine, upstream_b, ROWS_ROWS),
        dot(scaled_other, upstream_b, ROWS_ROWS).astype(BF16),
    )
    _, post_pull = jax.vjp(post_norm, mixed.astype(F32), gate, gain_out)
    grad_mixed, grad_gate, grad_gain_out = post_pull(grad_scaled)
    grad_gate = grad_gate.astype(BF16)
    dy = grad_mixed.astype(BF16).astype(F32)
    dy_cum = dy * cum_w
    a_term = dot(c, dy_cum, ROWS_ROWS)
    a_out = carried(a_term, decay, -1)
    du_inside, dgram, pair_rows, pair_cols = within_back(u, dy, cum, b, c, head_size)
    grad_c = dot(dy_cum, entering, COLS_COLS) + dot(dgram, b, ROWS_COLS)
    grad_b = dot(u * end_w, a_out, COLS_COLS) + dot(dgram, c, ROWS_ROWS)
    du_state = end_w * dot(b, a_out, ROWS_COLS)
    moved = narrow(du_state * u)
    decay_grad = jnp.sum(a_out * entering, axis=0, keepdims=True) * decay
    grad_last = jnp.sum(moved, axis=0, keepdims=True) + jnp.dot(
        decay_grad, widen.T, precision=HIGH
    )
    grad_cum = pair_rows - pair_cols.T + narrow(dy * across) - moved
    grad_log = lax.dot_general(tri, grad_cum, (ROWS_ROWS, ((), ())), precision=HIGH) + grad_last
    du = du_inside + du_state
    grad_xs = du * delta_w + skip_w * dy
    grad_delta = grad_log * rate + narrow(du * xs)
    grad_a_log = jnp.sum(grad_log * delta, axis=0) * rate
    grad_skip = jnp.dot(jnp.sum(dy * xs, axis=0), widen.T, precision=HIGH)
    grad_dt_raw = grad_delta * jax.nn.sigmoid(dt_raw + dt_bias)
    grad_dt_bias = jnp.sum(grad_dt_raw, axis=0)
    sig = jax.nn.sigmoid(pre)
    grad_pre = jnp.concatenate([grad_xs, grad_b, grad_c], axis=1) * sig * (1.0 + pre * (1.0 - sig))
    halo = shifted(grad_pre[: taps - 1].astype(BF16), "seq", -1).astype(F32)
    grad_padded = jnp.concatenate([grad_pre, halo], axis=0)
    grad_v = sum(
        conv_weight[k] * grad_padded[taps - 1 - k : taps - 1 - k + length] for k in range(taps)
    )
    grad_conv_weight = jnp.stack(
        [jnp.sum(grad_pre * padded[k : k + length], axis=0) for k in range(taps)]
    )
    grad_conv_bias = jnp.sum(grad_pre, axis=0)
    grad_rest = jnp.concatenate([grad_v.astype(BF16), grad_dt_raw.astype(BF16)], axis=1)
    grad_normed = join_halves(
        dot(grad_gate, win_mine[0], COLS_COLS) + dot(grad_rest, win_mine[1], COLS_COLS),
        dot(grad_gate, win_other[0], COLS_COLS) + dot(grad_rest, win_other[1], COLS_COLS),
        parts,
        first,
    )
    grad_win = tuple(
        (dot(normed_mine, part, ROWS_ROWS), dot(normed_other, part, ROWS_ROWS).astype(BF16))
        for part in (grad_gate, grad_rest)
    )
    _, norm_pull = jax.vjp(rms_scale, hidden, gain_in)
    grad_hidden, grad_gain_in = norm_pull(grad_normed)
    grad_small = (
        grad_conv_weight, grad_conv_bias, grad_a_log, grad_dt_bias, grad_skip, grad_gain_in,
        grad_gain_out,
    )
    return (upstream_b.astype(F32) + grad_hidden).astype(BF16), grad_win, grad_wout, grad_small


def both_cores(grad):
    mine, other = grad
    return (mine + swapped(other).astype(F32)).astype(BF16)


def reduced_ahead(both):
    return lax.psum(lax.psum_scatter(both, "wt", scatter_dimension=0, tiled=True), "seq")


def reduced_last(gate, rest, out):
    order = bits_of("wt")
    wide = LANES * (rest.shape[1] // (2 * LANES))
    gate = scatter_rows(gate, "wt", order)
    out = scatter_rows(out, "wt", order[::-1])
    rows = gate.shape[0]
    pieces = [gate] + [out[k : k + rows] for k in range(0, out.shape[0], rows)]
    early = sum_rows(jnp.concatenate(pieces, axis=1), "seq")
    late = jnp.concatenate(
        [
            scatter_rows(rest[:, :wide], "wt", order),
            scatter_rows(rest[:, wide:], "wt", order[::-1]),
        ],
        axis=1,
    )
    late = sum_rows(late, "seq")
    inner = gate.shape[1]
    columns = out.shape[1]
    total_in = jnp.concatenate([early[:, :inner], late], axis=1)
    total_out = jnp.concatenate(
        [early[:, at : at + columns] for at in range(inner, early.shape[1], columns)], axis=0
    )
    return total_in, total_out


def own_layer(layers, first):
    recv0 = lax.ppermute(layers[0], "section", [(1, 0)])
    recv1 = lax.ppermute(layers[1], "section", [(0, 1)])
    own = jnp.where(first, layers[0], layers[1])
    recv = jnp.where(first, recv0, recv1)
    joined = jnp.concatenate([jnp.where(first, own, recv), jnp.where(first, recv, own)], axis=0)
    return joined.astype(F32)[None]


def by_layer(results, first):
    own = jnp.where(first, results[0], results[1])
    recv = swapped(jnp.where(first, results[1], results[0]))
    return jnp.stack([jnp.where(first, own, recv), jnp.where(first, recv, own)])[None, :, None]


def local(tokens, cotangent, in_weight, out_weight, *small_shards):
    section = lax.axis_index("section")
    first = section == 0
    wt_id = lax.axis_index("wt")
    parts = lax.axis_size("wt")

    def halves(weight):
        rows = weight.shape[1] // 2
        keep = lax.dynamic_slice_in_dim(weight[0], section * rows, rows, 0)
        recv = swapped(lax.dynamic_slice_in_dim(weight[0], (1 - section) * rows, rows, 0))
        return jnp.where(first, keep, recv), jnp.where(first, recv, keep)

    inner = out_weight.shape[1] * parts
    order = bits_of("wt")

    def gathered(half):
        mine = lax.all_gather(half, "wt", axis=0, tiled=True)
        return mine, swapped(mine)

    def columns(pair):
        return tuple((whole[:, :inner], whole[:, inner:]) for whole in pair)

    win_halves, wout_halves = halves(in_weight), halves(out_weight)
    flat = jnp.concatenate([shard[0].reshape(-1) for shard in small_shards])
    packed = gather_rows(gather_rows(flat[None], "wt", order), "section", [1])
    packed = packed.reshape(2, parts, -1).astype(F32)
    smalls = []
    for layer in range(2):
        rest, small = packed[layer], []
        for shard in small_shards:
            shape = shard.shape[1:]
            size = shard[0].size
            piece, rest = rest[:, :size], rest[:, size:]
            if len(shape) == 2:
                piece = piece.reshape((parts,) + shape).swapaxes(0, 1)
                small.append(piece.reshape(shape[0], -1))
            else:
                small.append(piece.reshape(-1))
        smalls.append(tuple(small))
    win0_mine = (
        gather_rows(win_halves[0][:, :inner], "wt", order[::-1]),
        gather_rows(win_halves[0][:, inner:], "wt", order),
    )
    win0 = (win0_mine, tuple(swapped(part) for part in win0_mine))
    wout0 = gathered(wout_halves[0])
    next_half, _ = lax.optimization_barrier((win_halves[1], wout0[0]))
    win1 = gathered(next_half)
    next_half, _ = lax.optimization_barrier((wout_halves[1], win1[0]))
    wout1 = gathered(next_half)
    weights = ((win0, wout0), (columns(win1), wout1))

    own_tokens = lax.dynamic_index_in_dim(tokens, section, 0, keepdims=False)[0]
    own_cotangent = lax.dynamic_index_in_dim(cotangent, section, 0, keepdims=False)[0]
    out0, saved0 = layer_forward(own_tokens, weights[0], smalls[0], first, parts)
    out1, saved1 = layer_forward(out0, weights[1], smalls[1], first, parts)
    states = by_layer((out0, out1), first)
    back1, gwin1, gwout1, gsmall1 = layer_backward(
        own_cotangent, saved1, weights[1], smalls[1], first, parts
    )
    both_wout1 = both_cores(gwout1)
    both_win1 = jnp.concatenate([both_cores(part) for part in gwin1], axis=1)
    back1, both_wout1, both_win1 = lax.optimization_barrier((back1, both_wout1, both_win1))
    sum_wout1, sum_win1 = reduced_ahead(both_wout1), reduced_ahead(both_win1)
    back0, gwin0, gwout0, gsmall0 = layer_backward(
        back1, saved0, weights[0], smalls[0], first, parts
    )
    sum_win0, sum_wout0 = reduced_last(
        both_cores(gwin0[0]), both_cores(gwin0[1]), both_cores(gwout0)
    )
    input_grads = by_layer((back0, back1), first)

    flat0 = jnp.concatenate([g.reshape(-1) for g in gsmall0])
    flat1 = jnp.concatenate([g.reshape(-1) for g in gsmall1])
    total = jnp.where(first, flat0, flat1) + swapped(jnp.where(first, flat1, flat0))
    for axis in ("wt", "seq"):
        for bit in bits_of(axis):
            total = total + crossed(total, axis, bit)
    small_out, at = [], 0
    for g in gsmall0:
        piece = total[at : at + g.size].reshape(g.shape)
        at += g.size
        axis = g.ndim - 1
        share = g.shape[axis] // parts
        small_out.append(lax.dynamic_slice_in_dim(piece, wt_id * share, share, axis)[None])
    return (
        states,
        input_grads,
        own_layer((sum_win0, sum_win1), first),
        own_layer((sum_wout0, sum_wout1), first),
        *small_out,
    )


def solution(mesh):
    shards = (
        P("section", "wt", None),
        P("section", "wt", None),
        P("section", None, "wt"),
        P("section", "wt"),
        P("section", "wt"),
        P("section", "wt"),
        P("section", "wt"),
        P("section", "wt"),
        P("section", "wt"),
    )
    return jax.shard_map(
        local,
        mesh=mesh,
        in_specs=(P(None, "wt", "seq", None), P(None, "wt", "seq", None)) + shards,
        out_specs=(P("section", None, "wt", "seq", None), P("section", None, "wt", "seq", None))
        + shards,
        check_vma=False,
    )
```

```python
import jax
import jax.numpy as jnp
from jax import lax
from jax.experimental import pallas as pl
from jax.experimental.pallas import tpu as pltpu
from jax.sharding import PartitionSpec as P

EPSILON = 1e-05
HIGH = lax.Precision.HIGHEST
F32 = jnp.float32
BF16 = jnp.bfloat16
LANES = 128


def shifted(block, axis, distance):
    devices = range(lax.axis_size(axis))
    route = [(i - distance, i) for i in devices if i - distance in devices]
    return lax.ppermute(block, axis, route)


def swapped(block):
    return lax.ppermute(block, "section", [(0, 1), (1, 0)])


def crossed(block, axis, bit):
    devices = range(lax.axis_size(axis))
    return lax.ppermute(block, axis, [(i, i ^ bit) for i in devices])


def bits_of(axis):
    count = lax.axis_size(axis)
    return [1 << k for k in range(count.bit_length() - 1)]


def has_bit(axis, bit):
    return (lax.axis_index(axis) // bit) % 2 == 1


def gather_rows(block, axis, order):
    rows, columns = block.shape
    done = []
    for bit in order:
        recv, high = crossed(block, axis, bit), has_bit(axis, bit)
        at = sum(1 for other in done if other > bit)
        block = jnp.stack([jnp.where(high, recv, block), jnp.where(high, block, recv)], axis=at)
        done.append(bit)
    return block.reshape(-1, columns)


def scatter_rows(total, axis, order):
    rows, columns = total.shape
    left = sorted(order, reverse=True)
    total = total.reshape((2,) * len(left) + (rows >> len(left), columns))
    for bit in order:
        at = left.index(bit)
        left.remove(bit)
        low = lax.index_in_dim(total, 0, at, keepdims=False)
        top = lax.index_in_dim(total, 1, at, keepdims=False)
        high = has_bit(axis, bit)
        recv = crossed(jnp.where(high, low, top), axis, bit)
        total = (jnp.where(high, top, low).astype(F32) + recv.astype(F32)).astype(BF16)
    return total


def sum_rows(total, axis):
    order = bits_of(axis)
    return gather_rows(scatter_rows(total, axis, order), axis, order[::-1])


def rms_scale(values, gain):
    return values * lax.rsqrt(jnp.mean(values * values, axis=-1, keepdims=True) + EPSILON) * gain


def post_norm(mixed, gate_part, gain_out):
    return rms_scale(mixed * jax.nn.silu(gate_part), gain_out)


def dot(a, b, over):
    return lax.dot_general(
        a.astype(BF16), b.astype(BF16), (over, ((), ())), preferred_element_type=F32
    )


ROWS_COLS = ((1,), (0,))
COLS_COLS = ((1,), (1,))
ROWS_ROWS = ((0,), (0,))


def head_decay(head, cum_ref, cum_t_ref):
    heads = lax.broadcasted_iota(jnp.int32, cum_ref.shape, 1)
    column = jnp.sum(jnp.where(heads == head, cum_ref[...], 0.0), axis=1, keepdims=True)
    row = cum_t_ref[pl.ds(head, 1), :]
    return jnp.exp(jnp.minimum(column - row, 0.0))


def causal_gram(c_ref, b_ref, gram):
    length = gram.shape[0]
    product = dot(c_ref[...], b_ref[...], COLS_COLS)
    rows = lax.broadcasted_iota(jnp.int32, (length, length), 0)
    cols = lax.broadcasted_iota(jnp.int32, (length, length), 1)
    gram[...] = jnp.where(rows >= cols, product, 0.0)


def within_kernel(head_size, u_ref, cum_ref, cum_t_ref, b_ref, c_ref, y_ref, gram):
    tile = pl.program_id(0)
    per_tile = LANES // head_size

    @pl.when(tile == 0)
    def _():
        causal_gram(c_ref, b_ref, gram)

    u = u_ref[...]
    owner = lax.broadcasted_iota(jnp.int32, u.shape, 1) // head_size
    total = jnp.zeros(u.shape, F32)
    for k in range(per_tile):
        weights = head_decay(tile * per_tile + k, cum_ref, cum_t_ref) * gram[...]
        total += dot(weights, jnp.where(owner == k, u, 0.0), ROWS_COLS)
    y_ref[...] = total


def within_back_kernel(
    head_size,
    u_ref,
    dy_ref,
    cum_ref,
    cum_t_ref,
    b_ref,
    c_ref,
    du_ref,
    dgram_ref,
    rows_ref,
    cols_ref,
    gram,
):
    tile = pl.program_id(0)
    per_tile = LANES // head_size

    @pl.when(tile == 0)
    def _():
        causal_gram(c_ref, b_ref, gram)
        dgram_ref[...] = jnp.zeros_like(dgram_ref)
        rows_ref[...] = jnp.zeros_like(rows_ref)

    u = u_ref[...].astype(BF16)
    dy = dy_ref[...]
    length = u.shape[0]
    owner = lax.broadcasted_iota(jnp.int32, dy.shape, 1) // head_size
    heads = lax.broadcasted_iota(jnp.int32, rows_ref.shape, 1)
    causal = lax.broadcasted_iota(jnp.int32, (length, length), 0) >= lax.broadcasted_iota(
        jnp.int32, (length, length), 1
    )
    total = jnp.zeros(dy.shape, F32)
    for k in range(per_tile):
        head = tile * per_tile + k
        decay = head_decay(head, cum_ref, cum_t_ref)
        weights = decay * gram[...]
        dy_own = jnp.where(owner == k, dy, 0.0).astype(BF16)
        dweights = dot(dy_own, u, COLS_COLS)
        dgram_ref[...] += jnp.where(causal, dweights * decay, 0.0)
        pairs = dweights * weights
        rows_ref[...] += jnp.where(heads == head, jnp.sum(pairs, axis=1, keepdims=True), 0.0)
        cols_ref[pl.ds(head, 1), :] = jnp.sum(pairs, axis=0, keepdims=True)
        total += dot(weights, dy_own, ROWS_ROWS)
    du_ref[...] = total


def full(shape):
    return pl.BlockSpec(shape, lambda i: (0,) * len(shape))


def within(u, cum, b, c, head_size):
    length, channels = u.shape
    cum_t = cum.T
    tile = pl.BlockSpec((length, LANES), lambda i: (0, i))
    return pl.pallas_call(
        lambda *refs: within_kernel(head_size, *refs),
        grid=(channels // LANES,),
        out_shape=jax.ShapeDtypeStruct(u.shape, F32),
        in_specs=[tile, full(cum.shape), full(cum_t.shape), full(b.shape), full(c.shape)],
        out_specs=tile,
        scratch_shapes=[pltpu.VMEM((length, length), F32)],
        cost_estimate=pl.CostEstimate(
            flops=length * length * channels * 8,
            bytes_accessed=8 * u.size,
            transcendentals=length * length * channels // head_size,
        ),
    )(u, cum, cum_t, b, c)


def within_back(u, dy, cum, b, c, head_size):
    length, channels = u.shape
    cum_t = cum.T
    tile = pl.BlockSpec((length, LANES), lambda i: (0, i))
    return pl.pallas_call(
        lambda *refs: within_back_kernel(head_size, *refs),
        grid=(channels // LANES,),
        out_shape=(
            jax.ShapeDtypeStruct(u.shape, F32),
            jax.ShapeDtypeStruct((length, length), F32),
            jax.ShapeDtypeStruct(cum.shape, F32),
            jax.ShapeDtypeStruct(cum_t.shape, F32),
        ),
        in_specs=[tile, tile, full(cum.shape), full(cum_t.shape), full(b.shape), full(c.shape)],
        out_specs=(tile, full((length, length)), full(cum.shape), full(cum_t.shape)),
        scratch_shapes=[pltpu.VMEM((length, length), F32)],
        cost_estimate=pl.CostEstimate(
            flops=length * length * channels * 16,
            bytes_accessed=12 * u.size,
            transcendentals=length * length * channels // head_size,
        ),
    )(u, dy, cum, cum_t, b, c)


def carried(term, decay, distance):
    count = lax.axis_size("seq")
    if count == 1:
        return jnp.zeros_like(term)
    state = shifted(term.astype(BF16), "seq", distance).astype(F32)
    for _ in range(count - 2):
        state = shifted((term + decay * state).astype(BF16), "seq", distance).astype(F32)
    return state


def split_halves(array, parts, first):
    share = array.shape[1] // (2 * parts)
    pieces = [array[:, j * share : (j + 1) * share] for j in range(2 * parts)]
    even = jnp.concatenate(pieces[0::2], axis=1)
    odd = jnp.concatenate(pieces[1::2], axis=1)
    return jnp.where(first, even, odd), jnp.where(first, odd, even)


def join_halves(mine, other, parts, first):
    even, odd = jnp.where(first, mine, other), jnp.where(first, other, mine)
    share = mine.shape[1] // parts
    pieces = []
    for j in range(parts):
        pieces += [even[:, j * share : (j + 1) * share], odd[:, j * share : (j + 1) * share]]
    return jnp.concatenate(pieces, axis=1)


def head_map(heads, channels):
    return (jnp.arange(channels)[None, :] // (channels // heads) == jnp.arange(heads)[:, None]).astype(F32)


def layer_forward(hidden_b, weights, small, first, parts):
    (win_mine, win_other), (wout_mine, wout_other) = weights
    conv_weight, conv_bias, a_log, dt_bias, d_skip, gain_in, gain_out = small
    heads, inner, conv = a_log.shape[0], gain_out.shape[0], conv_bias.shape[0]
    head_size = inner // heads
    state_size = (conv - inner) // 2
    taps = conv_weight.shape[0]
    hidden = hidden_b.astype(F32)
    length = hidden.shape[0]
    normed = rms_scale(hidden, gain_in).astype(BF16)
    normed_mine, normed_other = split_halves(normed, parts, first)
    gate, project = (
        dot(normed_mine, mine, ROWS_COLS) + dot(normed_other, other, ROWS_COLS)
        for mine, other in zip(win_mine, win_other)
    )
    v = project[:, :conv].astype(BF16)
    dt_raw = project[:, conv:].astype(BF16).astype(F32)
    halo = shifted(v[length - taps + 1 :], "seq", 1)
    padded = jnp.concatenate([halo, v], axis=0).astype(F32)
    pre = conv_bias
    for k in range(taps):
        pre = pre + conv_weight[k] * padded[k : k + length]
    conv_out = jax.nn.silu(pre)
    xs = conv_out[:, :inner]
    b = conv_out[:, inner : inner + state_size]
    c = conv_out[:, inner + state_size :]
    delta = jax.nn.softplus(dt_raw + dt_bias)
    rate = -jnp.exp(a_log)
    tri = jnp.tril(jnp.ones((length, length), F32))
    cum = jnp.dot(tri, delta * rate, precision=HIGH)
    last = cum[length - 1 :]
    widen = head_map(heads, inner)
    delta_w = jnp.dot(delta, widen, precision=HIGH)
    cum_w = jnp.dot(jnp.exp(cum), widen, precision=HIGH)
    end_w = jnp.dot(jnp.exp(last - cum), widen, precision=HIGH)
    decay = cum_w[length - 1 :]
    skip_w = jnp.repeat(d_skip, head_size)
    u = xs * delta_w
    term = dot(b, u * end_w, ROWS_ROWS)
    entering = carried(term, decay, 1)
    inside = within(u, cum, b, c, head_size)
    across = cum_w * dot(c, entering, ROWS_COLS)
    mixed = (inside + across + skip_w * xs).astype(BF16)
    scaled = post_norm(mixed.astype(F32), gate, gain_out).astype(BF16)
    scaled_mine, scaled_other = split_halves(scaled, parts, first)
    output = (
        hidden
        + dot(scaled_mine, wout_mine, ROWS_COLS)
        + dot(scaled_other, wout_other, ROWS_COLS)
    )
    saved = (
        hidden, normed_mine, normed_other, gate, padded, dt_raw, pre, xs, b, c, delta, rate, tri,
        cum, widen, delta_w, cum_w, end_w, decay, skip_w, u, entering, across, mixed,
        scaled_mine, scaled_other,
    )
    return output.astype(BF16), saved


def layer_backward(upstream_b, saved, weights, small, first, parts):
    (win_mine, win_other), (wout_mine, wout_other) = weights
    conv_weight, conv_bias, a_log, dt_bias, d_skip, gain_in, gain_out = small
    (
        hidden, normed_mine, normed_other, gate, padded, dt_raw, pre, xs, b, c, delta, rate, tri,
        cum, widen, delta_w, cum_w, end_w, decay, skip_w, u, entering, across, mixed,
        scaled_mine, scaled_other,
    ) = saved
    heads, inner = a_log.shape[0], gain_out.shape[0]
    head_size = inner // heads
    taps = conv_weight.shape[0]
    length = hidden.shape[0]

    def narrow(array):
        return dot(array, widen, COLS_COLS)

    grad_scaled = join_halves(
        dot(upstream_b, wout_mine, COLS_COLS), dot(upstream_b, wout_other, COLS_COLS), parts, first
    )
    grad_wout = (
        dot(scaled_mine, upstream_b, ROWS_ROWS),
        dot(scaled_other, upstream_b, ROWS_ROWS).astype(BF16),
    )
    _, post_pull = jax.vjp(post_norm, mixed.astype(F32), gate, gain_out)
    grad_mixed, grad_gate, grad_gain_out = post_pull(grad_scaled)
    grad_gate = grad_gate.astype(BF16)
    dy = grad_mixed.astype(BF16).astype(F32)
    dy_cum = dy * cum_w
    a_term = dot(c, dy_cum, ROWS_ROWS)
    a_out = carried(a_term, decay, -1)
    du_inside, dgram, pair_rows, pair_cols = within_back(u, dy, cum, b, c, head_size)
    grad_c = dot(dy_cum, entering, COLS_COLS) + dot(dgram, b, ROWS_COLS)
    grad_b = dot(u * end_w, a_out, COLS_COLS) + dot(dgram, c, ROWS_ROWS)
    du_state = end_w * dot(b, a_out, ROWS_COLS)
    moved = narrow(du_state * u)
    decay_grad = jnp.sum(a_out * entering, axis=0, keepdims=True) * decay
    grad_last = jnp.sum(moved, axis=0, keepdims=True) + jnp.dot(
        decay_grad, widen.T, precision=HIGH
    )
    grad_cum = pair_rows - pair_cols.T + narrow(dy * across) - moved
    grad_log = lax.dot_general(tri, grad_cum, (ROWS_ROWS, ((), ())), precision=HIGH) + grad_last
    du = du_inside + du_state
    grad_xs = du * delta_w + skip_w * dy
    grad_delta = grad_log * rate + narrow(du * xs)
    grad_a_log = jnp.sum(grad_log * delta, axis=0) * rate
    grad_skip = jnp.dot(jnp.sum(dy * xs, axis=0), widen.T, precision=HIGH)
    grad_dt_raw = grad_delta * jax.nn.sigmoid(dt_raw + dt_bias)
    grad_dt_bias = jnp.sum(grad_dt_raw, axis=0)
    sig = jax.nn.sigmoid(pre)
    grad_pre = jnp.concatenate([grad_xs, grad_b, grad_c], axis=1) * sig * (1.0 + pre * (1.0 - sig))
    halo = shifted(grad_pre[: taps - 1].astype(BF16), "seq", -1).astype(F32)
    grad_padded = jnp.concatenate([grad_pre, halo], axis=0)
    grad_v = sum(
        conv_weight[k] * grad_padded[taps - 1 - k : taps - 1 - k + length] for k in range(taps)
    )
    grad_conv_weight = jnp.stack(
        [jnp.sum(grad_pre * padded[k : k + length], axis=0) for k in range(taps)]
    )
    grad_conv_bias = jnp.sum(grad_pre, axis=0)
    grad_rest = jnp.concatenate([grad_v.astype(BF16), grad_dt_raw.astype(BF16)], axis=1)
    grad_normed = join_halves(
        dot(grad_gate, win_mine[0], COLS_COLS) + dot(grad_rest, win_mine[1], COLS_COLS),
        dot(grad_gate, win_other[0], COLS_COLS) + dot(grad_rest, win_other[1], COLS_COLS),
        parts,
        first,
    )
    grad_win = tuple(
        (dot(normed_mine, part, ROWS_ROWS), dot(normed_other, part, ROWS_ROWS).astype(BF16))
        for part in (grad_gate, grad_rest)
    )
    _, norm_pull = jax.vjp(rms_scale, hidden, gain_in)
    grad_hidden, grad_gain_in = norm_pull(grad_normed)
    grad_small = (
        grad_conv_weight, grad_conv_bias, grad_a_log, grad_dt_bias, grad_skip, grad_gain_in,
        grad_gain_out,
    )
    return (upstream_b.astype(F32) + grad_hidden).astype(BF16), grad_win, grad_wout, grad_small


def both_cores(grad):
    mine, other = grad
    return (mine + swapped(other).astype(F32)).astype(BF16)


def reduced(gate, rest, out):
    order = bits_of("wt")
    wide = LANES * (rest.shape[1] // (2 * LANES))
    gate = scatter_rows(gate, "wt", order)
    out = scatter_rows(out, "wt", order[::-1])
    rows = gate.shape[0]
    pieces = [gate] + [out[k : k + rows] for k in range(0, out.shape[0], rows)]
    early = sum_rows(jnp.concatenate(pieces, axis=1), "seq")
    late = jnp.concatenate(
        [
            scatter_rows(rest[:, :wide], "wt", order),
            scatter_rows(rest[:, wide:], "wt", order[::-1]),
        ],
        axis=1,
    )
    late = sum_rows(late, "seq")
    inner = gate.shape[1]
    columns = out.shape[1]
    total_in = jnp.concatenate([early[:, :inner], late], axis=1)
    total_out = jnp.concatenate(
        [early[:, at : at + columns] for at in range(inner, early.shape[1], columns)], axis=0
    )
    return total_in, total_out


def own_layer(layers, first):
    recv0 = lax.ppermute(layers[0], "section", [(1, 0)])
    recv1 = lax.ppermute(layers[1], "section", [(0, 1)])
    own = jnp.where(first, layers[0], layers[1])
    recv = jnp.where(first, recv0, recv1)
    joined = jnp.concatenate([jnp.where(first, own, recv), jnp.where(first, recv, own)], axis=0)
    return joined.astype(F32)[None]


def by_layer(results, first):
    own = jnp.where(first, results[0], results[1])
    recv = swapped(jnp.where(first, results[1], results[0]))
    return jnp.stack([jnp.where(first, own, recv), jnp.where(first, recv, own)])[None, :, None]


def local(tokens, cotangent, in_weight, out_weight, *small_shards):
    section = lax.axis_index("section")
    first = section == 0
    wt_id = lax.axis_index("wt")
    parts = lax.axis_size("wt")

    def halves(weight):
        rows = weight.shape[1] // 2
        keep = lax.dynamic_slice_in_dim(weight[0], section * rows, rows, 0)
        recv = swapped(lax.dynamic_slice_in_dim(weight[0], (1 - section) * rows, rows, 0))
        return jnp.where(first, keep, recv), jnp.where(first, recv, keep)

    inner = out_weight.shape[1] * parts
    order = bits_of("wt")

    def gathered(half):
        mine = lax.all_gather(half, "wt", axis=0, tiled=True)
        return mine, swapped(mine)

    def columns(pair):
        return tuple((whole[:, :inner], whole[:, inner:]) for whole in pair)

    win_halves, wout_halves = halves(in_weight), halves(out_weight)
    flat = jnp.concatenate([shard[0].reshape(-1) for shard in small_shards])
    packed = gather_rows(gather_rows(flat[None], "wt", order), "section", [1])
    packed = packed.reshape(2, parts, -1).astype(F32)
    smalls = []
    for layer in range(2):
        rest, small = packed[layer], []
        for shard in small_shards:
            shape = shard.shape[1:]
            size = shard[0].size
            piece, rest = rest[:, :size], rest[:, size:]
            if len(shape) == 2:
                piece = piece.reshape((parts,) + shape).swapaxes(0, 1)
                small.append(piece.reshape(shape[0], -1))
            else:
                small.append(piece.reshape(-1))
        smalls.append(tuple(small))
    win0_mine = (
        gather_rows(win_halves[0][:, :inner], "wt", order[::-1]),
        gather_rows(win_halves[0][:, inner:], "wt", order),
    )
    win0 = (win0_mine, tuple(swapped(part) for part in win0_mine))
    next_half, _ = lax.optimization_barrier((wout_halves[0], win0_mine))
    wout0 = gathered(next_half)
    next_half, _ = lax.optimization_barrier((win_halves[1], wout0[0]))
    win1 = gathered(next_half)
    next_half, _ = lax.optimization_barrier((wout_halves[1], win1[0]))
    wout1 = gathered(next_half)
    weights = ((win0, wout0), (columns(win1), wout1))

    own_tokens = lax.dynamic_index_in_dim(tokens, section, 0, keepdims=False)[0]
    own_cotangent = lax.dynamic_index_in_dim(cotangent, section, 0, keepdims=False)[0]
    out0, saved0 = layer_forward(own_tokens, weights[0], smalls[0], first, parts)
    out1, saved1 = layer_forward(out0, weights[1], smalls[1], first, parts)
    states = by_layer((out0, out1), first)
    back1, gwin1, gwout1, gsmall1 = layer_backward(
        own_cotangent, saved1, weights[1], smalls[1], first, parts
    )
    both1 = (both_cores(gwin1[0]), both_cores(gwin1[1]), both_cores(gwout1))
    back1, both1 = lax.optimization_barrier((back1, both1))
    sum_win1, sum_wout1 = reduced(*both1)
    back0, gwin0, gwout0, gsmall0 = layer_backward(
        back1, saved0, weights[0], smalls[0], first, parts
    )
    sum_win0, sum_wout0 = reduced(
        both_cores(gwin0[0]), both_cores(gwin0[1]), both_cores(gwout0)
    )
    input_grads = by_layer((back0, back1), first)

    flat0 = jnp.concatenate([g.reshape(-1) for g in gsmall0])
    flat1 = jnp.concatenate([g.reshape(-1) for g in gsmall1])
    total = jnp.where(first, flat0, flat1) + swapped(jnp.where(first, flat1, flat0))
    for axis in ("wt", "seq"):
        for bit in bits_of(axis):
            total = total + crossed(total, axis, bit)
    small_out, at = [], 0
    for g in gsmall0:
        piece = total[at : at + g.size].reshape(g.shape)
        at += g.size
        axis = g.ndim - 1
        share = g.shape[axis] // parts
        small_out.append(lax.dynamic_slice_in_dim(piece, wt_id * share, share, axis)[None])
    return (
        states,
        input_grads,
        own_layer((sum_win0, sum_win1), first),
        own_layer((sum_wout0, sum_wout1), first),
        *small_out,
    )


def solution(mesh):
    shards = (
        P("section", "wt", None),
        P("section", "wt", None),
        P("section", None, "wt"),
        P("section", "wt"),
        P("section", "wt"),
        P("section", "wt"),
        P("section", "wt"),
        P("section", "wt"),
        P("section", "wt"),
    )
    return jax.shard_map(
        local,
        mesh=mesh,
        in_specs=(P(None, "wt", "seq", None), P(None, "wt", "seq", None)) + shards,
        out_specs=(P("section", None, "wt", "seq", None), P("section", None, "wt", "seq", None))
        + shards,
        check_vma=False,
    )
```
